32 devices in a mesh: grp: 2 (over y), chol: 4 (over z), orb: 4 (over x, core).
Axes of the slice: x: 2, y: 2, z: 4, core: 2. Of those that a mesh axis runs over, the one named last changes fastest.
Arguments:
- green: bfloat16 [32, 600, 896], P(('grp', 'chol'), None, 'orb'), parts along dimension 0, may hold values from -6 to 6
- half_chol: bfloat16 [80, 600, 896], P(('grp', 'chol'), None, 'orb'), parts along dimension 0, may hold values from -0.0078125 to 0.0078125
- chol_vec: bfloat16 [80, 896, 896], P(('grp', 'chol'), 'orb'), parts along dimension 0, may hold values from -0.0546875 to 0.0546875
- noise: float32 [32, 40], P('grp', 'chol'), parts along dimension 0, may hold values from -6 to 6
- order: int32 [32], P('grp'), parts along dimension 0, may hold values from 0 to 15, each once
- walkers: bfloat16 [32, 600, 896], P(('grp', 'chol'), None, 'orb'), parts along dimension 0, may hold values from -3 to 3
Outputs:
- force_bias: float32 [32, 40], P('grp', 'chol'), parts along dimension 0
- propagated: bfloat16 [32, 600, 896], P(('grp', 'chol'), None, 'orb'), parts along dimension 0
The draws below stay inside these ranges and needn't reach their ends.
There are 2 independent parts, one for each index of `grp`. The reference program is written for one: setup_inputs(seed, part) draws one part's arguments, and reference() takes and returns one part's arrays. A program takes and returns all parts, laid end to end along the dimension named above; each array names one. Nothing has to cross between parts.
Inputs may be any that keep to these rules, and one draw needn't show every extreme that they name: order is a permutation of the 16 walkers.
All inputs are finite; a program needn't handle non-finite values.
Results may differ from the reference program's by a relative error of at most 0.0086.
Values may be sent and summed in bfloat16 or wider, within the bound.
A program may use at most 64 MiB of HBM per device.

```python
import jax
import jax.numpy as jnp

M = 896
NOCC = 600
W = 16
TERMS = 6
CHOL = 40


def steps_of(own_key, dims, shards, low, top_value):
    def one(position, blocks):
        draws = jax.random.uniform(jax.random.fold_in(jax.random.fold_in(own_key, 6), position), (blocks,), jnp.float32, low / len(shards), top_value / len(shards))
        return jnp.repeat(jnp.exp(draws), dims[position] // blocks).reshape((-1,) + (1,) * (len(dims) - position - 1))

    factor_of = one(*shards[0])
    for cut in shards[1:]:
        factor_of = factor_of * one(*cut)
    return factor_of


def normal_values(key, shape, scale, reach, pieces=(), kind=jnp.bfloat16):
    gain = steps_of(key, shape, pieces, -0.22, 0.18) if pieces else 1.0
    drawn = jax.random.normal(key, shape, jnp.float32) * scale * gain
    return jnp.minimum(jnp.maximum(drawn, -reach), reach).astype(kind)


def setup_inputs(seed: int = 0, part: int = 0) -> dict:
    arg_keys = jax.random.split(jax.random.key(seed), 7)
    part_splits = jax.random.split(jax.random.fold_in(arg_keys[6], part), 7)
    return {
        "green": normal_values(part_splits[0], (W, NOCC, M), 1.0, 6.0, ((0, 4), (2, 4))),
        "half_chol": normal_values(part_splits[1], (CHOL, NOCC, M), (NOCC * M) ** -0.5, 0.0078125, ((0, 4), (2, 4))),
        "chol_vec": normal_values(part_splits[2], (CHOL, M, M), (CHOL * M // 3) ** -0.5, 0.0546875, ((0, 4), (1, 4))),
        "noise": normal_values(part_splits[3], (W, CHOL), 1.0, 6.0, ((1, 4),), jnp.float32),
        "order": jax.random.permutation(part_splits[4], W).astype(jnp.int32),
        "walkers": normal_values(part_splits[5], (W, NOCC, M), 0.5, 3.0, ((0, 4), (2, 4))),
    }


def reference(green, half_chol, chol_vec, noise, order, walkers):
    chosen = jnp.take(green, order, axis=0)
    force_bias = jnp.dot(chosen.reshape(W, NOCC * M), half_chol.reshape(CHOL, NOCC * M).T, preferred_element_type=jnp.float32)
    fields = (noise - force_bias).astype(jnp.bfloat16)
    summed = jnp.dot(fields.astype(jnp.float32), chol_vec.reshape(CHOL, M * M).astype(jnp.float32), preferred_element_type=jnp.float32)
    propagator = summed.astype(jnp.bfloat16).reshape(W, M, M)
    prop_wide = propagator.astype(jnp.float32)
    running = walkers.astype(jnp.float32)
    term_now = walkers
    for power in range(1, TERMS + 1):
        scaled = jnp.einsum("wiq,wpq->wip", term_now.astype(jnp.float32), prop_wide, preferred_element_type=jnp.float32) / power
        running = running + scaled
        term_now = scaled.astype(jnp.bfloat16)
    return force_bias, running.astype(jnp.bfloat16)
```

```python
import jax
import jax.numpy as jnp
from jax import lax
from jax.sharding import PartitionSpec as P

TERMS = 6


def ring(n):
    return [(i, (i + 1) % n) for i in range(n)]


def force_of(green, half_chol):
    n = lax.axis_size("chol")
    me = lax.axis_index("chol")
    each = green.shape[0]
    values = jnp.zeros((n * each, half_chol.shape[0]), jnp.float32)
    block = green
    for step in range(n):
        later = lax.ppermute(block, "chol", ring(n)) if step < n - 1 else None
        part = jnp.einsum("wiq,giq->wg", block, half_chol, preferred_element_type=jnp.float32)
        owner = lax.rem(me - step + n, n)
        values = lax.dynamic_update_slice(values, part, (owner * each, 0))
        block = later
    return values


def summed_rows(fields, chol_vec, each, chunks):
    n = lax.axis_size("chol")
    me = lax.axis_index("chol")
    size = each // chunks
    done = [None] * chunks
    for step in range(n):
        owner = lax.rem(me - step - 1 + 2 * n, n)
        for c in range(chunks):
            mine = lax.dynamic_slice(
                fields, (owner * each + c * size, 0), (size, fields.shape[1])
            )
            part = jnp.einsum("wg,gpq->wpq", mine, chol_vec, preferred_element_type=jnp.float32)
            if done[c] is not None:
                part = part + done[c].astype(jnp.float32)
            part = part.astype(jnp.bfloat16)
            done[c] = lax.ppermute(part, "chol", ring(n)) if step < n - 1 else part
    return done


def body(green, half_chol, chol_vec, noise, order, walkers):
    each = walkers.shape[0]
    orb = lax.axis_size("orb")
    by_walker = each % orb == 0
    split = 0 if by_walker else 1
    held = lax.all_to_all(walkers, "orb", split_axis=split, concat_axis=2, tiled=True)

    values = lax.psum(force_of(green, half_chol), "orb")
    force_bias = jnp.take(values, order, axis=0)
    fields = (noise - force_bias).astype(jnp.bfloat16)
    chunks = 2 if each % 2 == 0 else 1
    rows = jnp.concatenate(summed_rows(fields, chol_vec, each, chunks), axis=0)
    if by_walker:
        prop = lax.all_to_all(rows, "orb", split_axis=0, concat_axis=1, tiled=True)
    else:
        prop = lax.all_gather(rows, "orb", axis=1, tiled=True)
    running = held.astype(jnp.float32)
    term_now = held
    for power in range(1, TERMS + 1):
        scaled = (
            jnp.einsum("wiq,wpq->wip", term_now, prop, preferred_element_type=jnp.float32)
            / power
        )
        running = running + scaled
        term_now = scaled.astype(jnp.bfloat16)
    propagated = lax.all_to_all(
        running.astype(jnp.bfloat16), "orb", split_axis=2, concat_axis=split, tiled=True
    )
    return (force_bias, propagated)


def solution(mesh):
    return jax.shard_map(
        body,
        mesh=mesh,
        in_specs=(
            P(("grp", "chol"), None, "orb"),
            P(("grp", "chol"), None, "orb"),
            P(("grp", "chol"), "orb", None),
            P("grp", "chol"),
            P("grp"),
            P(("grp", "chol"), None, "orb"),
        ),
        out_specs=(P("grp", "chol"), P(("grp", "chol"), None, "orb")),
        check_vma=False,
    )
```

```python
import jax
import jax.numpy as jnp
from jax import lax
from jax.experimental import pallas as pl
from jax.experimental.pallas import tpu as pltpu
from jax.sharding import PartitionSpec as P

TERMS = 6


def ring(n):
    return [(i, (i + 1) % n) for i in range(n)]


def force_of(green, half_chol):
    n = lax.axis_size("chol")
    me = lax.axis_index("chol")
    each = green.shape[0]
    values = jnp.zeros((n * each, half_chol.shape[0]), jnp.float32)
    block = green
    for step in range(n):
        later = lax.ppermute(block, "chol", ring(n)) if step < n - 1 else None
        part = jnp.einsum("wiq,giq->wg", block, half_chol, preferred_element_type=jnp.float32)
        owner = lax.rem(me - step + n, n)
        values = lax.dynamic_update_slice(values, part, (owner * each, 0))
        block = later
    return values


def summed_rows(fields, chol_vec, each, chunks):
    n = lax.axis_size("chol")
    me = lax.axis_index("chol")
    size = each // chunks
    done = [None] * chunks
    for step in range(n):
        owner = lax.rem(me - step - 1 + 2 * n, n)
        for c in range(chunks):
            mine = lax.dynamic_slice(
                fields, (owner * each + c * size, 0), (size, fields.shape[1])
            )
            part = jnp.einsum("wg,gpq->wpq", mine, chol_vec, preferred_element_type=jnp.float32)
            if done[c] is not None:
                part = part + done[c].astype(jnp.float32)
            part = part.astype(jnp.bfloat16)
            done[c] = lax.ppermute(part, "chol", ring(n)) if step < n - 1 else part
    return done


def rows_of(fields, chol_vec, start, size):
    mine = lax.dynamic_slice(fields, (start, 0), (size, fields.shape[1]))
    return jnp.einsum("wg,gpq->wpq", mine, chol_vec, preferred_element_type=jnp.float32)


def line_of_four(green, half_chol, chol_vec, noise, order, each, chunks):
    me = lax.axis_index("chol")
    inner = jnp.logical_and(me >= 1, me <= 2)

    def go(array, pairs):
        return lax.ppermute(array, "chol", pairs)

    r1 = go(green, [(0, 1), (1, 2), (2, 3)])
    l1 = go(green, [(1, 0), (2, 1), (3, 2)])
    r2 = go(r1, [(1, 2), (2, 3)])
    l2 = go(l1, [(2, 1), (1, 0)])
    r3 = go(r2, [(2, 3)])
    l3 = go(l2, [(1, 0)])
    high = chol_vec.shape[1] // chunks
    own_chol, far_chol = [], []
    after = (r1, l1)
    for c in range(chunks):
        part = chol_vec[:, c * high : (c + 1) * high]
        own_chol.append(part)
        held_back = lax.optimization_barrier((part,) + after)[0]
        got = go(held_back, [(0, 1), (3, 2)])
        far_chol.append(got)
        after = (got,)

    values = jnp.zeros((4 * each, half_chol.shape[0]), jnp.float32)
    for block, owner in (
        (green, me),
        (l1 + r3, (me + 1) % 4),
        (r2 + l2, (me + 2) % 4),
        (r1 + l3, (me + 3) % 4),
    ):
        part = jnp.einsum("wiq,giq->wg", block, half_chol, preferred_element_type=jnp.float32)
        values = lax.dynamic_update_slice(values, part, (owner * each, 0))
    values = lax.psum(values, "orb")
    force_bias = jnp.take(values, order, axis=0)
    fields = (noise - force_bias).astype(jnp.bfloat16)
    end_fields = go(fields, [(0, 1), (3, 2)])

    near = jnp.where(me <= 1, 0, 3) * each
    far = jnp.where(me <= 1, 3, 0) * each
    across = jnp.where(me <= 1, 2, 1) * each
    rows = []
    for c in range(chunks):
        def share(start):
            return rows_of(fields, own_chol[c], start, each) + rows_of(
                end_fields, far_chol[c], start, each
            )

        first = go(share(far).astype(jnp.bfloat16), [(1, 2), (2, 1)])
        second = go(share(across).astype(jnp.bfloat16), [(1, 2), (2, 1)])
        ends = (first.astype(jnp.float32) + share(near)).astype(jnp.bfloat16)
        ends = go(ends, [(1, 0), (2, 3)])
        own = (second.astype(jnp.float32) + share(me * each)).astype(jnp.bfloat16)
        rows.append(jnp.where(inner, own, ends))
    return force_bias, rows


def taylor_kernel(held_ref, prop_ref, out_ref, term, running):
    parts, _, wide = held_ref.shape
    for j in range(parts):
        cols = slice(j * wide, (j + 1) * wide)
        term[0, :, cols] = held_ref[j]
        running[:, cols] = held_ref[j].astype(jnp.float32)
    total = parts * wide

    def step(now, later, factor):
        for low in range(0, total, 256):
            cols = slice(low, min(low + 256, total))
            scaled = (
                lax.dot_general(
                    term[now],
                    prop_ref[cols, :],
                    (((1,), (1,)), ((), ())),
                    preferred_element_type=jnp.float32,
                )
                * factor
            )
            running[:, cols] += scaled
            term[later, :, cols] = scaled.astype(jnp.bfloat16)

    for power in range(1, TERMS + 1):
        step((power - 1) % 2, power % 2, 1.0 / power)
    for j in range(parts):
        out_ref[j] = running[:, j * wide : (j + 1) * wide].astype(out_ref.dtype)


def taylor(held, prop):
    parts, tall, wide = held.shape
    return pl.pallas_call(
        taylor_kernel,
        out_shape=jax.ShapeDtypeStruct(held.shape, held.dtype),
        in_specs=[pl.BlockSpec(memory_space=pltpu.VMEM)] * 2,
        out_specs=pl.BlockSpec(memory_space=pltpu.VMEM),
        scratch_shapes=[
            pltpu.VMEM((2, tall, parts * wide), jnp.bfloat16),
            pltpu.VMEM((tall, parts * wide), jnp.float32),
        ],
        compiler_params=pltpu.CompilerParams(vmem_limit_bytes=40 * 2**20),
        cost_estimate=pl.CostEstimate(
            flops=2 * TERMS * tall * (parts * wide) ** 2,
            bytes_accessed=6 * tall * parts * wide,
            transcendentals=0,
        ),
    )(held, prop)


def body(green, half_chol, chol_vec, noise, order, walkers):
    each = walkers.shape[0]
    orb = lax.axis_size("orb")
    whole = each == orb
    if whole:
        held = lax.all_to_all(walkers, "orb", split_axis=0, concat_axis=0, tiled=True)
    else:
        held = lax.all_to_all(walkers, "orb", split_axis=1, concat_axis=2, tiled=True)

    if lax.axis_size("chol") == 4:
        force_bias, rows = line_of_four(
            green, half_chol, chol_vec, noise, order, each, 2 if whole else 1
        )
    else:
        values = lax.psum(force_of(green, half_chol), "orb")
        force_bias = jnp.take(values, order, axis=0)
        fields = (noise - force_bias).astype(jnp.bfloat16)
        chunks = 2 if each % 2 == 0 else 1
        rows = [jnp.concatenate(summed_rows(fields, chol_vec, each, chunks), axis=0)]
    if whole:
        arrived = [
            lax.all_to_all(part, "orb", split_axis=0, concat_axis=0, tiled=True) for part in rows
        ]
        prop = jnp.concatenate(arrived, axis=1)
        prop = prop.reshape(-1, prop.shape[2])
        blocks = taylor(held, prop)
        propagated = lax.all_to_all(blocks, "orb", split_axis=0, concat_axis=0, tiled=True)
        return (force_bias, propagated)
    prop = lax.all_gather(jnp.concatenate(rows, axis=1), "orb", axis=1, tiled=True)
    running = held.astype(jnp.float32)
    term_now = held
    for power in range(1, TERMS + 1):
        scaled = (
            jnp.einsum("wiq,wpq->wip", term_now, prop, preferred_element_type=jnp.float32)
            / power
        )
        running = running + scaled
        term_now = scaled.astype(jnp.bfloat16)
    propagated = lax.all_to_all(
        running.astype(jnp.bfloat16), "orb", split_axis=2, concat_axis=1, tiled=True
    )
    return (force_bias, propagated)


def solution(mesh):
    return jax.shard_map(
        body,
        mesh=mesh,
        in_specs=(
            P(("grp", "chol"), None, "orb"),
            P(("grp", "chol"), None, "orb"),
            P(("grp", "chol"), "orb", None),
            P("grp", "chol"),
            P("grp"),
            P(("grp", "chol"), None, "orb"),
        ),
        out_specs=(P("grp", "chol"), P(("grp", "chol"), None, "orb")),
        check_vma=False,
    )
```

```python
import jax
import jax.numpy as jnp
from jax import lax
from jax.experimental import pallas as pl
from jax.experimental.pallas import tpu as pltpu
from jax.sharding import PartitionSpec as P

TERMS = 6


def ring(n):
    return [(i, (i + 1) % n) for i in range(n)]


def force_of(green, half_chol):
    n = lax.axis_size("chol")
    me = lax.axis_index("chol")
    each = green.shape[0]
    values = jnp.zeros((n * each, half_chol.shape[0]), jnp.float32)
    block = green
    for step in range(n):
        later = lax.ppermute(block, "chol", ring(n)) if step < n - 1 else None
        part = jnp.einsum("wiq,giq->wg", block, half_chol, preferred_element_type=jnp.float32)
        owner = lax.rem(me - step + n, n)
        values = lax.dynamic_update_slice(values, part, (owner * each, 0))
        block = later
    return values


def summed_rows(fields, chol_vec, each, chunks):
    n = lax.axis_size("chol")
    me = lax.axis_index("chol")
    size = each // chunks
    done = [None] * chunks
    for step in range(n):
        owner = lax.rem(me - step - 1 + 2 * n, n)
        for c in range(chunks):
            mine = lax.dynamic_slice(
                fields, (owner * each + c * size, 0), (size, fields.shape[1])
            )
            part = jnp.einsum("wg,gpq->wpq", mine, chol_vec, preferred_element_type=jnp.float32)
            if done[c] is not None:
                part = part + done[c].astype(jnp.float32)
            part = part.astype(jnp.bfloat16)
            done[c] = lax.ppermute(part, "chol", ring(n)) if step < n - 1 else part
    return done


def rows_of(fields, chol_vec, start, size):
    mine = lax.dynamic_slice(fields, (start, 0), (size, fields.shape[1]))
    return jnp.einsum("wg,gpq->wpq", mine, chol_vec, preferred_element_type=jnp.float32)


def line_of_four(green, half_chol, chol_vec, noise, order, each, chunks):
    me = lax.axis_index("chol")
    inner = jnp.logical_and(me >= 1, me <= 2)

    def go(array, pairs):
        return lax.ppermute(array, "chol", pairs)

    r1 = go(green, [(0, 1), (1, 2), (2, 3)])
    l1 = go(green, [(1, 0), (2, 1), (3, 2)])
    r2 = go(r1, [(1, 2), (2, 3)])
    l2 = go(l1, [(2, 1), (1, 0)])
    r3 = go(r2, [(2, 3)])
    l3 = go(l2, [(1, 0)])
    high = chol_vec.shape[1] // chunks
    own_chol, far_chol = [], []
    after = (r2,)
    for c in range(chunks):
        part = chol_vec[:, c * high : (c + 1) * high]
        own_chol.append(part)
        held_back = lax.optimization_barrier((part,) + after)[0]
        got = go(held_back, [(0, 1), (3, 2)])
        far_chol.append(got)
        after = (got,)

    values = jnp.zeros((4 * each, half_chol.shape[0]), jnp.float32)
    for block, owner in (
        (green, me),
        (l1 + r3, (me + 1) % 4),
        (r2 + l2, (me + 2) % 4),
        (r1 + l3, (me + 3) % 4),
    ):
        part = jnp.einsum("wiq,giq->wg", block, half_chol, preferred_element_type=jnp.float32)
        values = lax.dynamic_update_slice(values, part, (owner * each, 0))
    values = lax.psum(values, "orb")
    force_bias = jnp.take(values, order, axis=0)
    fields = (noise - force_bias).astype(jnp.bfloat16)
    end_fields = go(fields, [(0, 1), (3, 2)])

    near = jnp.where(me <= 1, 0, 3) * each
    far = jnp.where(me <= 1, 3, 0) * each
    across = jnp.where(me <= 1, 2, 1) * each
    rows = []
    for c in range(chunks):
        def share(start):
            return rows_of(fields, own_chol[c], start, each) + rows_of(
                end_fields, far_chol[c], start, each
            )

        first = go(share(far).astype(jnp.bfloat16), [(1, 2), (2, 1)])
        second = go(share(across).astype(jnp.bfloat16), [(1, 2), (2, 1)])
        ends = (first.astype(jnp.float32) + share(near)).astype(jnp.bfloat16)
        ends = go(ends, [(1, 0), (2, 3)])
        own = (second.astype(jnp.float32) + share(me * each)).astype(jnp.bfloat16)
        rows.append(jnp.where(inner, own, ends))
    return force_bias, rows


def taylor_kernel(held_ref, prop_ref, out_ref, term, running):
    parts, _, wide = held_ref.shape
    for j in range(parts):
        cols = slice(j * wide, (j + 1) * wide)
        term[0, :, cols] = held_ref[j]
        running[:, cols] = held_ref[j].astype(jnp.float32)
    total = parts * wide

    def step(now, later, factor):
        for low in range(0, total, 256):
            cols = slice(low, min(low + 256, total))
            scaled = (
                lax.dot_general(
                    term[now],
                    prop_ref[cols, :],
                    (((1,), (1,)), ((), ())),
                    preferred_element_type=jnp.float32,
                )
                * factor
            )
            running[:, cols] += scaled
            term[later, :, cols] = scaled.astype(jnp.bfloat16)

    for power in range(1, TERMS + 1):
        step((power - 1) % 2, power % 2, 1.0 / power)
    for j in range(parts):
        out_ref[j] = running[:, j * wide : (j + 1) * wide].astype(out_ref.dtype)


def taylor(held, prop):
    parts, tall, wide = held.shape
    return pl.pallas_call(
        taylor_kernel,
        out_shape=jax.ShapeDtypeStruct(held.shape, held.dtype),
        in_specs=[pl.BlockSpec(memory_space=pltpu.VMEM)] * 2,
        out_specs=pl.BlockSpec(memory_space=pltpu.VMEM),
        scratch_shapes=[
            pltpu.VMEM((2, tall, parts * wide), jnp.bfloat16),
            pltpu.VMEM((tall, parts * wide), jnp.float32),
        ],
        compiler_params=pltpu.CompilerParams(vmem_limit_bytes=40 * 2**20),
        cost_estimate=pl.CostEstimate(
            flops=2 * TERMS * tall * (parts * wide) ** 2,
            bytes_accessed=6 * tall * parts * wide,
            transcendentals=0,
        ),
    )(held, prop)


def body(green, half_chol, chol_vec, noise, order, walkers):
    each = walkers.shape[0]
    orb = lax.axis_size("orb")
    whole = each == orb
    if whole:
        held = lax.all_to_all(walkers, "orb", split_axis=0, concat_axis=0, tiled=True)
    else:
        held = lax.all_to_all(walkers, "orb", split_axis=1, concat_axis=2, tiled=True)

    if lax.axis_size("chol") == 4:
        force_bias, rows = line_of_four(
            green, half_chol, chol_vec, noise, order, each, 2 if whole else 1
        )
    else:
        values = lax.psum(force_of(green, half_chol), "orb")
        force_bias = jnp.take(values, order, axis=0)
        fields = (noise - force_bias).astype(jnp.bfloat16)
        chunks = 2 if each % 2 == 0 else 1
        rows = [jnp.concatenate(summed_rows(fields, chol_vec, each, chunks), axis=0)]
    if whole:
        arrived = [
            lax.all_to_all(part, "orb", split_axis=0, concat_axis=0, tiled=True) for part in rows
        ]
        prop = jnp.concatenate(arrived, axis=1)
        prop = prop.reshape(-1, prop.shape[2])
        blocks = taylor(held, prop)
        propagated = lax.all_to_all(blocks, "orb", split_axis=0, concat_axis=0, tiled=True)
        return (force_bias, propagated)
    prop = lax.all_gather(jnp.concatenate(rows, axis=1), "orb", axis=1, tiled=True)
    running = held.astype(jnp.float32)
    term_now = held
    for power in range(1, TERMS + 1):
        scaled = (
            jnp.einsum("wiq,wpq->wip", term_now, prop, preferred_element_type=jnp.float32)
            / power
        )
        running = running + scaled
        term_now = scaled.astype(jnp.bfloat16)
    propagated = lax.all_to_all(
        running.astype(jnp.bfloat16), "orb", split_axis=2, concat_axis=1, tiled=True
    )
    return (force_bias, propagated)


def solution(mesh):
    return jax.shard_map(
        body,
        mesh=mesh,
        in_specs=(
            P(("grp", "chol"), None, "orb"),
            P(("grp", "chol"), None, "orb"),
            P(("grp", "chol"), "orb", None),
            P("grp", "chol"),
            P("grp"),
            P(("grp", "chol"), None, "orb"),
        ),
        out_specs=(P("grp", "chol"), P(("grp", "chol"), None, "orb")),
        check_vma=False,
    )
```

```python
import jax
import jax.numpy as jnp
from jax import lax
from jax.experimental import pallas as pl
from jax.experimental.pallas import tpu as pltpu
from jax.sharding import PartitionSpec as P

TERMS = 6


def ring(n):
    return [(i, (i + 1) % n) for i in range(n)]


def force_of(green, half_chol):
    n = lax.axis_size("chol")
    me = lax.axis_index("chol")
    each = green.shape[0]
    values = jnp.zeros((n * each, half_chol.shape[0]), jnp.float32)
    block = green
    for step in range(n):
        later = lax.ppermute(block, "chol", ring(n)) if step < n - 1 else None
        part = jnp.einsum("wiq,giq->wg", block, half_chol, preferred_element_type=jnp.float32)
        owner = lax.rem(me - step + n, n)
        values = lax.dynamic_update_slice(values, part, (owner * each, 0))
        block = later
    return values


def summed_rows(fields, chol_vec, each, chunks):
    n = lax.axis_size("chol")
    me = lax.axis_index("chol")
    size = each // chunks
    done = [None] * chunks
    for step in range(n):
        owner = lax.rem(me - step - 1 + 2 * n, n)
        for c in range(chunks):
            mine = lax.dynamic_slice(
                fields, (owner * each + c * size, 0), (size, fields.shape[1])
            )
            part = jnp.einsum("wg,gpq->wpq", mine, chol_vec, preferred_element_type=jnp.float32)
            if done[c] is not None:
                part = part + done[c].astype(jnp.float32)
            part = part.astype(jnp.bfloat16)
            done[c] = lax.ppermute(part, "chol", ring(n)) if step < n - 1 else part
    return done


def rows_of(fields, chol_vec, start, size):
    mine = lax.dynamic_slice(fields, (start, 0), (size, fields.shape[1]))
    return jnp.einsum("wg,gpq->wpq", mine, chol_vec, preferred_element_type=jnp.float32)


def line_of_four(green, half_chol, chol_vec, noise, order, each, chunks):
    me = lax.axis_index("chol")
    inner = jnp.logical_and(me >= 1, me <= 2)

    def go(array, pairs):
        return lax.ppermute(array, "chol", pairs)

    r1 = go(green, [(0, 1), (1, 2), (2, 3)])
    l1 = go(green, [(1, 0), (2, 1), (3, 2)])
    r2 = go(r1, [(1, 2), (2, 3)])
    l2 = go(l1, [(2, 1), (1, 0)])
    r3 = go(r2, [(2, 3)])
    l3 = go(l2, [(1, 0)])
    high = chol_vec.shape[1] // chunks
    own_chol, far_chol = [], []
    after = (r1,)
    for c in range(chunks):
        part = chol_vec[:, c * high : (c + 1) * high]
        own_chol.append(part)
        held_back = lax.optimization_barrier((part,) + after)[0]
        got = go(held_back, [(0, 1), (3, 2)])
        far_chol.append(got)
        after = (got,)

    values = jnp.zeros((4 * each, half_chol.shape[0]), jnp.float32)
    for block, owner in (
        (green, me),
        (l1 + r3, (me + 1) % 4),
        (r2 + l2, (me + 2) % 4),
        (r1 + l3, (me + 3) % 4),
    ):
        part = jnp.einsum("wiq,giq->wg", block, half_chol, preferred_element_type=jnp.float32)
        values = lax.dynamic_update_slice(values, part, (owner * each, 0))
    values = lax.psum(values, "orb")
    force_bias = jnp.take(values, order, axis=0)
    fields = (noise - force_bias).astype(jnp.bfloat16)
    end_fields = go(fields, [(0, 1), (3, 2)])

    near = jnp.where(me <= 1, 0, 3) * each
    far = jnp.where(me <= 1, 3, 0) * each
    across = jnp.where(me <= 1, 2, 1) * each
    rows = []
    for c in range(chunks):
        def share(start):
            return rows_of(fields, own_chol[c], start, each) + rows_of(
                end_fields, far_chol[c], start, each
            )

        first = go(share(far).astype(jnp.bfloat16), [(1, 2), (2, 1)])
        second = go(share(across).astype(jnp.bfloat16), [(1, 2), (2, 1)])
        ends = (first.astype(jnp.float32) + share(near)).astype(jnp.bfloat16)
        ends = go(ends, [(1, 0), (2, 3)])
        own = (second.astype(jnp.float32) + share(me * each)).astype(jnp.bfloat16)
        rows.append(jnp.where(inner, own, ends))
    return force_bias, rows


def taylor_kernel(held_ref, prop_ref, out_ref, term, running):
    parts, _, wide = held_ref.shape
    for j in range(parts):
        cols = slice(j * wide, (j + 1) * wide)
        term[0, :, cols] = held_ref[j]
        running[:, cols] = held_ref[j].astype(jnp.float32)
    total = parts * wide

    def step(now, later, factor):
        for low in range(0, total, 256):
            cols = slice(low, min(low + 256, total))
            scaled = (
                lax.dot_general(
                    term[now],
                    prop_ref[cols, :],
                    (((1,), (1,)), ((), ())),
                    preferred_element_type=jnp.float32,
                )
                * factor
            )
            running[:, cols] += scaled
            term[later, :, cols] = scaled.astype(jnp.bfloat16)

    for power in range(1, TERMS + 1):
        step((power - 1) % 2, power % 2, 1.0 / power)
    for j in range(parts):
        out_ref[j] = running[:, j * wide : (j + 1) * wide].astype(out_ref.dtype)


def taylor(held, prop):
    parts, tall, wide = held.shape
    return pl.pallas_call(
        taylor_kernel,
        out_shape=jax.ShapeDtypeStruct(held.shape, held.dtype),
        in_specs=[pl.BlockSpec(memory_space=pltpu.VMEM)] * 2,
        out_specs=pl.BlockSpec(memory_space=pltpu.VMEM),
        scratch_shapes=[
            pltpu.VMEM((2, tall, parts * wide), jnp.bfloat16),
            pltpu.VMEM((tall, parts * wide), jnp.float32),
        ],
        compiler_params=pltpu.CompilerParams(vmem_limit_bytes=40 * 2**20),
        cost_estimate=pl.CostEstimate(
            flops=2 * TERMS * tall * (parts * wide) ** 2,
            bytes_accessed=6 * tall * parts * wide,
            transcendentals=0,
        ),
    )(held, prop)


def body(green, half_chol, chol_vec, noise, order, walkers):
    each = walkers.shape[0]
    orb = lax.axis_size("orb")
    whole = each == orb
    if whole:
        held = lax.all_to_all(walkers, "orb", split_axis=0, concat_axis=0, tiled=True)
    else:
        held = lax.all_to_all(walkers, "orb", split_axis=1, concat_axis=2, tiled=True)

    if lax.axis_size("chol") == 4:
        force_bias, rows = line_of_four(
            green, half_chol, chol_vec, noise, order, each, 2 if whole else 1
        )
    else:
        values = lax.psum(force_of(green, half_chol), "orb")
        force_bias = jnp.take(values, order, axis=0)
        fields = (noise - force_bias).astype(jnp.bfloat16)
        chunks = 2 if each % 2 == 0 else 1
        rows = [jnp.concatenate(summed_rows(fields, chol_vec, each, chunks), axis=0)]
    if whole:
        arrived = [
            lax.all_to_all(part, "orb", split_axis=0, concat_axis=0, tiled=True) for part in rows
        ]
        prop = jnp.concatenate(arrived, axis=1)
        prop = prop.reshape(-1, prop.shape[2])
        blocks = taylor(held, prop)
        propagated = lax.all_to_all(blocks, "orb", split_axis=0, concat_axis=0, tiled=True)
        return (force_bias, propagated)
    prop = lax.all_gather(jnp.concatenate(rows, axis=1), "orb", axis=1, tiled=True)
    running = held.astype(jnp.float32)
    term_now = held
    for power in range(1, TERMS + 1):
        scaled = (
            jnp.einsum("wiq,wpq->wip", term_now, prop, preferred_element_type=jnp.float32)
            / power
        )
        running = running + scaled
        term_now = scaled.astype(jnp.bfloat16)
    propagated = lax.all_to_all(
        running.astype(jnp.bfloat16), "orb", split_axis=2, concat_axis=1, tiled=True
    )
    return (force_bias, propagated)


def solution(mesh):
    return jax.shard_map(
        body,
        mesh=mesh,
        in_specs=(
            P(("grp", "chol"), None, "orb"),
            P(("grp", "chol"), None, "orb"),
            P(("grp", "chol"), "orb", None),
            P("grp", "chol"),
            P("grp"),
            P(("grp", "chol"), None, "orb"),
        ),
        out_specs=(P("grp", "chol"), P(("grp", "chol"), None, "orb")),
        check_vma=False,
    )
```

```python
import jax
import jax.numpy as jnp
from jax import lax
from jax.experimental import pallas as pl
from jax.experimental.pallas import tpu as pltpu
from jax.sharding import PartitionSpec as P

TERMS = 6


def ring(n):
    return [(i, (i + 1) % n) for i in range(n)]


def force_of(green, half_chol):
    n = lax.axis_size("chol")
    me = lax.axis_index("chol")
    each = green.shape[0]
    values = jnp.zeros((n * each, half_chol.shape[0]), jnp.float32)
    block = green
    for step in range(n):
        later = lax.ppermute(block, "chol", ring(n)) if step < n - 1 else None
        part = jnp.einsum("wiq,giq->wg", block, half_chol, preferred_element_type=jnp.float32)
        owner = lax.rem(me - step + n, n)
        values = lax.dynamic_update_slice(values, part, (owner * each, 0))
        block = later
    return values


def summed_rows(fields, chol_vec, each, chunks):
    n = lax.axis_size("chol")
    me = lax.axis_index("chol")
    size = each // chunks
    done = [None] * chunks
    for step in range(n):
        owner = lax.rem(me - step - 1 + 2 * n, n)
        for c in range(chunks):
            mine = lax.dynamic_slice(
                fields, (owner * each + c * size, 0), (size, fields.shape[1])
            )
            part = jnp.einsum("wg,gpq->wpq", mine, chol_vec, preferred_element_type=jnp.float32)
            if done[c] is not None:
                part = part + done[c].astype(jnp.float32)
            part = part.astype(jnp.bfloat16)
            done[c] = lax.ppermute(part, "chol", ring(n)) if step < n - 1 else part
    return done


def rows_of(fields, chol_vec, start, size):
    mine = lax.dynamic_slice(fields, (start, 0), (size, fields.shape[1]))
    return jnp.einsum("wg,gpq->wpq", mine, chol_vec, preferred_element_type=jnp.float32)


def line_of_four(green, half_chol, chol_vec, noise, order, each, chunks):
    me = lax.axis_index("chol")
    inner = jnp.logical_and(me >= 1, me <= 2)

    def go(array, pairs):
        return lax.ppermute(array, "chol", pairs)

    r1 = go(green, [(0, 1), (1, 2), (2, 3)])
    l1 = go(green, [(1, 0), (2, 1), (3, 2)])
    r2 = go(r1, [(1, 2), (2, 3)])
    l2 = go(l1, [(2, 1), (1, 0)])
    r3 = go(r2, [(2, 3)])
    l3 = go(l2, [(1, 0)])
    tall = chol_vec.shape[1]
    edges = [0, tall] if chunks == 1 else [0, -(-tall * 5 // 8 // 16) * 16, tall]
    own_chol, far_chol = [], []
    after = (r1,)
    for c in range(chunks):
        part = chol_vec[:, edges[c] : edges[c + 1]]
        own_chol.append(part)
        held_back = lax.optimization_barrier((part,) + after)[0]
        got = go(held_back, [(0, 1), (3, 2)])
        far_chol.append(got)
        after = (got,)

    values = jnp.zeros((4 * each, half_chol.shape[0]), jnp.float32)
    for block, owner in (
        (green, me),
        (l1 + r3, (me + 1) % 4),
        (r2 + l2, (me + 2) % 4),
        (r1 + l3, (me + 3) % 4),
    ):
        part = jnp.einsum("wiq,giq->wg", block, half_chol, preferred_element_type=jnp.float32)
        values = lax.dynamic_update_slice(values, part, (owner * each, 0))
    values = lax.psum(values, "orb")
    force_bias = jnp.take(values, order, axis=0)
    fields = (noise - force_bias).astype(jnp.bfloat16)
    end_fields = go(fields, [(0, 1), (3, 2)])

    near = jnp.where(me <= 1, 0, 3) * each
    far = jnp.where(me <= 1, 3, 0) * each
    across = jnp.where(me <= 1, 2, 1) * each
    rows = []
    for c in range(chunks):
        def share(start):
            return rows_of(fields, own_chol[c], start, each) + rows_of(
                end_fields, far_chol[c], start, each
            )

        first = go(share(far).astype(jnp.bfloat16), [(1, 2), (2, 1)])
        second = go(share(across).astype(jnp.bfloat16), [(1, 2), (2, 1)])
        ends = (first.astype(jnp.float32) + share(near)).astype(jnp.bfloat16)
        ends = go(ends, [(1, 0), (2, 3)])
        own = (second.astype(jnp.float32) + share(me * each)).astype(jnp.bfloat16)
        rows.append(jnp.where(inner, own, ends))
    return force_bias, rows


def taylor_kernel(held_ref, prop_ref, out_ref, term, running):
    parts, _, wide = held_ref.shape
    for j in range(parts):
        cols = slice(j * wide, (j + 1) * wide)
        term[0, :, cols] = held_ref[j]
        running[:, cols] = held_ref[j].astype(jnp.float32)
    total = parts * wide

    def step(now, later, factor):
        for low in range(0, total, 256):
            cols = slice(low, min(low + 256, total))
            scaled = (
                lax.dot_general(
                    term[now],
                    prop_ref[cols, :],
                    (((1,), (1,)), ((), ())),
                    preferred_element_type=jnp.float32,
                )
                * factor
            )
            running[:, cols] += scaled
            term[later, :, cols] = scaled.astype(jnp.bfloat16)

    for power in range(1, TERMS + 1):
        step((power - 1) % 2, power % 2, 1.0 / power)
    for j in range(parts):
        out_ref[j] = running[:, j * wide : (j + 1) * wide].astype(out_ref.dtype)


def taylor(held, prop):
    parts, tall, wide = held.shape
    return pl.pallas_call(
        taylor_kernel,
        out_shape=jax.ShapeDtypeStruct(held.shape, held.dtype),
        in_specs=[pl.BlockSpec(memory_space=pltpu.VMEM)] * 2,
        out_specs=pl.BlockSpec(memory_space=pltpu.VMEM),
        scratch_shapes=[
            pltpu.VMEM((2, tall, parts * wide), jnp.bfloat16),
            pltpu.VMEM((tall, parts * wide), jnp.float32),
        ],
        compiler_params=pltpu.CompilerParams(vmem_limit_bytes=40 * 2**20),
        cost_estimate=pl.CostEstimate(
            flops=2 * TERMS * tall * (parts * wide) ** 2,
            bytes_accessed=6 * tall * parts * wide,
            transcendentals=0,
        ),
    )(held, prop)


def body(green, half_chol, chol_vec, noise, order, walkers):
    each = walkers.shape[0]
    orb = lax.axis_size("orb")
    whole = each == orb
    if whole:
        held = lax.all_to_all(walkers, "orb", split_axis=0, concat_axis=0, tiled=True)
    else:
        held = lax.all_to_all(walkers, "orb", split_axis=1, concat_axis=2, tiled=True)

    if lax.axis_size("chol") == 4:
        force_bias, rows = line_of_four(
            green, half_chol, chol_vec, noise, order, each, 2 if whole else 1
        )
    else:
        values = lax.psum(force_of(green, half_chol), "orb")
        force_bias = jnp.take(values, order, axis=0)
        fields = (noise - force_bias).astype(jnp.bfloat16)
        chunks = 2 if each % 2 == 0 else 1
        rows = [jnp.concatenate(summed_rows(fields, chol_vec, each, chunks), axis=0)]
    if whole:
        arrived = [
            lax.all_to_all(part, "orb", split_axis=0, concat_axis=0, tiled=True) for part in rows
        ]
        prop = jnp.concatenate(arrived, axis=1)
        prop = prop.reshape(-1, prop.shape[2])
        blocks = taylor(held, prop)
        propagated = lax.all_to_all(blocks, "orb", split_axis=0, concat_axis=0, tiled=True)
        return (force_bias, propagated)
    prop = lax.all_gather(jnp.concatenate(rows, axis=1), "orb", axis=1, tiled=True)
    running = held.astype(jnp.float32)
    term_now = held
    for power in range(1, TERMS + 1):
        scaled = (
            jnp.einsum("wiq,wpq->wip", term_now, prop, preferred_element_type=jnp.float32)
            / power
        )
        running = running + scaled
        term_now = scaled.astype(jnp.bfloat16)
    propagated = lax.all_to_all(
        running.astype(jnp.bfloat16), "orb", split_axis=2, concat_axis=1, tiled=True
    )
    return (force_bias, propagated)


def solution(mesh):
    return jax.shard_map(
        body,
        mesh=mesh,
        in_specs=(
            P(("grp", "chol"), None, "orb"),
            P(("grp", "chol"), None, "orb"),
            P(("grp", "chol"), "orb", None),
            P("grp", "chol"),
            P("grp"),
            P(("grp", "chol"), None, "orb"),
        ),
        out_specs=(P("grp", "chol"), P(("grp", "chol"), None, "orb")),
        check_vma=False,
    )
```
